256 devices in a mesh: grp: 2 (over core), seq: 32 (over z, y), rep: 4 (over x).
Axes of the slice: x: 4, y: 4, z: 8, core: 2. Of those that a mesh axis runs over, the one named last changes fastest.
Arguments:
- qkv: bfloat16 [2, 16384, 3, 4096], P('grp', ('rep', 'seq')), parts along dimension 1, may hold values from -40 to 40
- hidden: bfloat16 [2, 16384, 4096], P('grp', ('rep', 'seq')), parts along dimension 1, may hold values from -6 to 6
- row_map: int32 [16384], P('rep'), parts along dimension 0, may hold values from 0 to 4095, as said below
- frame_flags: int32 [16], P('rep'), parts along dimension 0, may hold values from 0 to 1, as said below
Outputs:
- block_outputs: bfloat16 [2, 16384, 4096], P('grp', ('rep', 'seq')), parts along dimension 1
The draws below stay inside these ranges and needn't reach their ends.
There are 4 independent parts, one for each index of `rep`. The reference program is written for one: setup_inputs(seed, part) draws one part's arguments, and reference() takes and returns one part's arrays. A program takes and returns all parts, laid end to end along the dimension named above; each array names one. Nothing has to cross between parts.
Inputs may be any that keep to these rules, and one draw needn't show every extreme that they name: The context block holds the window frame-alternated: every token t with the same t mod 32 lies on one context device (which device holds which residue class varies by prompt), in a rotated order within the device. So row_map is a permutation, and each run of 128 context rows that one device holds sends exactly 4 rows into each run of 128 main rows that one device holds. `frame_flags`: exactly half of the frames are 1.
All inputs are finite; a program needn't handle non-finite values.
Results may differ from the reference program's by a relative error of at most 0.0031.
Values may be sent and summed in bfloat16 or wider, within the bound.
A program may use at most 64 MiB of HBM per device.

```python
import jax
import jax.numpy as jnp
from jax import lax

HEAD_DIM = 128
HEADS = 32
D = 4096
FRAMES = 4
TOK_DEV = 128
TOKENS = 4096
PEERS = 32


def draw_qkv(key, part):
    key = jax.random.fold_in(key, 11)
    first = jax.random.fold_in(key, 0)
    second = jax.random.fold_in(key, 1)
    sixth = jax.random.fold_in(key, 5)
    shape = (2, TOKENS, D)
    queries = 2.5 * jax.random.normal(first, shape, jnp.float32)
    key_rows = jax.random.normal(second, shape, jnp.float32)
    value_rows = jax.random.normal(sixth, shape, jnp.float32)
    return jnp.stack([queries, key_rows, value_rows], axis=2).astype(jnp.bfloat16)


def draw_row_map(key, part):
    key = jax.random.fold_in(key, 5)
    first, second = jax.random.split(key)
    residue = jax.random.permutation(first, PEERS)
    rotation = jax.random.randint(second, (PEERS,), 0, TOK_DEV)
    slot = jnp.arange(TOK_DEV)
    stride_index = (slot[None, :] + rotation[:, None]) % TOK_DEV
    target = stride_index * PEERS + residue[:, None]
    return target.reshape(TOKENS).astype(jnp.int32)


def draw_frame_flags(key, part):
    key = jax.random.fold_in(key, 7)
    return (jax.random.permutation(key, FRAMES) % 2).astype(jnp.int32)


def levels(key, extent, shards, least, largest):
    level = 1.0
    for dim, shards_of in shards:
        steps = jax.random.uniform(jax.random.fold_in(jax.random.fold_in(key, 6), dim), (shards_of,), jnp.float32, least / len(shards), largest / len(shards))
        level = level * jnp.repeat(jnp.exp(steps), extent[dim] // shards_of).reshape((-1,) + (1,) * (len(extent) - 1 - dim))
    return level


def scatter_about(own_key, extent, scale, most, cuts=(), held_as=jnp.bfloat16):
    values = scale * jax.random.normal(own_key, extent, jnp.float32)
    if cuts:
        values = values * levels(own_key, extent, cuts, -0.22, 0.18)
    return jnp.clip(values, -most, most).astype(held_as)


def setup_inputs(seed: int = 0, part: int = 0) -> dict:
    key_list = jax.random.split(jax.random.key(seed), 5)
    own_keys = jax.random.split(jax.random.fold_in(key_list[4], part), 5)
    qkv = draw_qkv(jax.random.fold_in(jax.random.fold_in(key_list[4], part), 71), part)
    hidden = scatter_about(own_keys[1], (2, TOKENS, D), 1.0, 6.0, ((0, 2), (1, 32)))
    row_map = draw_row_map(jax.random.fold_in(jax.random.fold_in(key_list[4], part), 71), part)
    frame_flags = draw_frame_flags(jax.random.fold_in(jax.random.fold_in(key_list[4], part), 71), part)
    return dict(qkv=qkv, hidden=hidden, row_map=row_map, frame_flags=frame_flags)


def attend_head(queries, key_rows, value_rows):
    scores = jnp.dot(queries, key_rows.T, preferred_element_type=jnp.float32) * (HEAD_DIM ** -0.5)
    highest = jnp.max(scores, axis=1, keepdims=True)
    weights = jnp.exp(scores - highest)
    totals = jnp.sum(weights, axis=1, keepdims=True)
    blended = jnp.dot(weights.astype(jnp.bfloat16), value_rows, preferred_element_type=jnp.float32)
    return (blended / totals).astype(jnp.bfloat16)


def attention(stacked):
    split_heads = stacked.reshape(TOKENS, 3, HEADS, HEAD_DIM).transpose(2, 1, 0, 3)
    result = lax.map(lambda triple: attend_head(triple[0], triple[1], triple[2]), split_heads)
    return result.transpose(1, 0, 2).reshape(TOKENS, D)


def reference(qkv, hidden, row_map, frame_flags):
    context_attended = attention(qkv[0])
    main_attended = attention(qkv[1])
    context_out = (hidden[0].astype(jnp.float32) + context_attended.astype(jnp.float32)).astype(jnp.bfloat16)
    hint = jnp.zeros_like(context_attended).at[row_map].set(context_attended)
    frame_of = (jnp.arange(TOKENS) // (TOKENS // FRAMES)).astype(jnp.int32)
    gate = frame_flags[frame_of].astype(jnp.float32)
    main_out = hidden[1].astype(jnp.float32) + main_attended.astype(jnp.float32)
    main_out = (main_out + gate[:, None] * hint.astype(jnp.float32)).astype(jnp.bfloat16)
    return jnp.stack([context_out, main_out])
```

```python
import math

import jax
import jax.numpy as jnp
from jax import lax
from jax.experimental import pallas as pl
from jax.experimental.pallas import tpu as pltpu
from jax.sharding import PartitionSpec as P

HEAD = 128
ROWS = 128
PEERS = 32
ZS = 8
YS = 4
TOKENS = ROWS * PEERS
FRAMES = 4
PAIR = 2
BLOCK = PAIR * ROWS
CHUNK = 512
SCALE = HEAD ** -0.5 * math.log2(math.e)
MESH = pl.DeviceIdType.MESH
LAST_DIMS = (((1,), (1,)), ((), ()))


def offset(step):
    turn = lax.rem(step, ZS)
    dz = jnp.where(lax.rem(turn, 2) == 1, ZS - (turn + 1) // 2, turn // 2)
    return dz, step // ZS


def ahead(me, step):
    dz, dy = offset(step)
    return lax.rem(me // YS + dz, ZS) * YS + lax.rem(lax.rem(me, YS) + dy, YS)


def behind(me, step):
    dz, dy = offset(step)
    return lax.rem(me // YS + ZS - dz, ZS) * YS + lax.rem(lax.rem(me, YS) + YS - dy, YS)


def columns(peer):
    return pl.ds(pl.multiple_of(peer * HEAD, HEAD), HEAD)


def attend(queries, keys, values, scores):
    highest = jnp.full((BLOCK, 128), -jnp.inf, jnp.float32)
    for start in range(0, TOKENS, CHUNK):
        part = lax.dot_general(
            queries, keys[pl.ds(start, CHUNK), :], LAST_DIMS, preferred_element_type=jnp.float32
        )
        scores[:, pl.ds(start, CHUNK)] = part
        for lane in range(0, CHUNK, 128):
            highest = jnp.maximum(highest, part[:, lane:lane + 128])
    highest = jnp.max(highest, axis=1, keepdims=True)
    totals = jnp.zeros((BLOCK, 128), jnp.float32)
    blended = jnp.zeros((BLOCK, HEAD), jnp.float32)
    for start in range(0, TOKENS, CHUNK):
        weights = jnp.exp2((scores[:, pl.ds(start, CHUNK)] - highest) * SCALE)
        for lane in range(0, CHUNK, 128):
            totals = totals + weights[:, lane:lane + 128]
        blended = blended + jnp.dot(
            weights.astype(jnp.bfloat16),
            values[pl.ds(start, CHUNK), :],
            preferred_element_type=jnp.float32,
        )
    return (blended / jnp.sum(totals, axis=1, keepdims=True)).astype(jnp.bfloat16)


def kernel(
    qkv, hidden, row_map, flags, out,
    keys, values, queries, scores, attended, hint, placed, landed, stream, map_rows, map_cells, owner_of,
    k_sent, k_got, v_sent, v_got, q_sent, q_got, back_sent, back_got, hint_sent, hint_got, local_sem,
):
    grp = lax.axis_index("grp")
    me = lax.axis_index("seq")

    def push(src, dst, sent, got, step, **device):
        return pltpu.make_async_remote_copy(
            src_ref=src, dst_ref=dst, send_sem=sent.at[step], recv_sem=got.at[step],
            device_id=device, device_id_type=MESH,
        )

    def key_copy(step):
        peer = ahead(me, step)
        return push(qkv.at[1, :, columns(peer)], keys.at[step], k_sent, k_got, step, seq=peer)

    def value_copy(step):
        peer = ahead(me, step)
        return push(qkv.at[2, :, columns(peer)], values.at[step], v_sent, v_got, step, seq=peer)

    def query_copy(step):
        peer = ahead(me, step)
        return push(qkv.at[0, :, columns(peer)], queries.at[step], q_sent, q_got, step, seq=peer)

    def back_copy(step):
        return push(attended.at[step], landed.at[step], back_sent, back_got, step, seq=behind(me, step))

    def hint_copy(step):
        return push(
            attended.at[step], hint.at[behind(me, step)], hint_sent, hint_got, step, grp=1 - grp
        )

    def each(first, last, body):
        def step(i, carry):
            body(i)
            return carry
        lax.fori_loop(first, last, step, 0)

    own = [
        pltpu.make_async_copy(qkv.at[1, :, columns(me)], keys.at[0], local_sem.at[0]),
        pltpu.make_async_copy(qkv.at[2, :, columns(me)], values.at[0], local_sem.at[1]),
        pltpu.make_async_copy(qkv.at[0, :, columns(me)], queries.at[0], local_sem.at[2]),
        pltpu.make_async_copy(hidden, stream, local_sem.at[3]),
        pltpu.make_async_copy(row_map, map_rows, local_sem.at[4]),
        pltpu.make_async_copy(row_map, map_cells, local_sem.at[5]),
    ]
    barrier = pltpu.get_barrier_semaphore()
    each(1, PEERS, lambda i: pl.semaphore_signal(
        barrier, inc=1, device_id={"seq": ahead(me, i)}, device_id_type=MESH))
    pl.semaphore_signal(barrier, inc=1, device_id={"grp": 1 - grp}, device_id_type=MESH)
    pl.semaphore_wait(barrier, PEERS)

    each(1, PEERS, lambda i: key_copy(i).start())
    each(1, PEERS, lambda i: value_copy(i).start())
    each(1, PEERS, lambda i: query_copy(i).start())
    for copy in own:
        copy.start()
    for copy in own:
        copy.wait()

    @pl.when(grp == 1)
    def _():
        def find(residue):
            def look(c, found):
                return jnp.where(lax.rem(map_cells[c, 0], PEERS) == residue, c, found)
            owner_of[residue] = lax.fori_loop(0, PEERS, look, 0)
        each(0, PEERS, find)

    each(1, PEERS, lambda i: key_copy(i).wait_recv())
    each(1, PEERS, lambda i: value_copy(i).wait_recv())

    flat_keys = keys.reshape(TOKENS, HEAD)
    flat_values = values.reshape(TOKENS, HEAD)

    def work(block):
        first = block * PAIR
        for step in (first, first + 1):
            @pl.when(step > 0)
            def _():
                query_copy(step).wait_recv()
        rows = queries[pl.ds(first, PAIR)].reshape(BLOCK, HEAD)
        result = attend(rows, flat_keys, flat_values, scores)
        attended[pl.ds(first, PAIR)] = result.reshape(PAIR, ROWS, HEAD)

        @pl.when(grp == 0)
        def _():
            for step in (first, first + 1):
                @pl.when(step > 0)
                def _():
                    back_copy(step).start()
                hint_copy(step).start()

    each(0, PEERS // PAIR, work)

    @pl.when(grp == 1)
    def _():
        each(0, PEERS, lambda i: hint_copy(i).wait_recv())

        def place(residue):
            source = owner_of[residue]
            spots = map_rows[pl.ds(source, 1), :] // PEERS
            chosen = lax.broadcasted_iota(jnp.int32, (ROWS, ROWS), 0) == spots
            rows = jnp.dot(
                chosen.astype(jnp.bfloat16), hint[source], preferred_element_type=jnp.float32
            )
            placed[pl.ds(residue, ROWS, stride=PEERS), :] = rows
        each(0, PEERS, place)

        def combine(step):
            token_peer = behind(me, step)
            gate = flags[token_peer // (PEERS // FRAMES)].astype(jnp.float32)
            rows = placed[pl.ds(pl.multiple_of(token_peer * ROWS, ROWS), ROWS), :]
            total = attended[step].astype(jnp.float32) + gate * rows
            attended[step] = total.astype(jnp.bfloat16)

            @pl.when(step > 0)
            def _():
                back_copy(step).start()
        each(0, PEERS, combine)

    each(1, PEERS, lambda i: key_copy(i).wait_send())
    each(1, PEERS, lambda i: value_copy(i).wait_send())
    each(1, PEERS, lambda i: query_copy(i).wait_send())

    def finish(step, rows):
        cols = columns(ahead(me, step))
        out[:, cols] = (stream[:, cols].astype(jnp.float32) + rows.astype(jnp.float32)).astype(jnp.bfloat16)

    finish(0, attended[0])

    def finish_landed(step):
        back_copy(step).wait_recv()
        finish(step, landed[step])
    each(1, PEERS, finish_landed)

    each(1, PEERS, lambda i: back_copy(i).wait_send())

    @pl.when(grp == 0)
    def _():
        each(0, PEERS, lambda i: hint_copy(i).wait_send())


def local(qkv, hidden, row_map, frame_flags):
    planes = jnp.transpose(qkv[0], (1, 0, 2))
    cells = row_map.reshape(PEERS, ROWS)
    wide = PEERS * HEAD
    pairs = PEERS * TOKENS * HEAD * ROWS
    sems = [pltpu.SemaphoreType.DMA((PEERS,))] * 10
    result = pl.pallas_call(
        kernel,
        out_shape=jax.ShapeDtypeStruct((ROWS, wide), jnp.bfloat16),
        in_specs=[
            pl.BlockSpec(memory_space=pl.ANY),
            pl.BlockSpec(memory_space=pl.ANY),
            pl.BlockSpec(memory_space=pl.ANY),
            pl.BlockSpec(memory_space=pltpu.SMEM),
        ],
        out_specs=pl.BlockSpec(memory_space=pltpu.VMEM),
        scratch_shapes=[
            pltpu.VMEM((PEERS, ROWS, HEAD), jnp.bfloat16),
            pltpu.VMEM((PEERS, ROWS, HEAD), jnp.bfloat16),
            pltpu.VMEM((PEERS, ROWS, HEAD), jnp.bfloat16),
            pltpu.VMEM((BLOCK, TOKENS), jnp.float32),
            pltpu.VMEM((PEERS, ROWS, HEAD), jnp.bfloat16),
            pltpu.VMEM((PEERS, ROWS, HEAD), jnp.bfloat16),
            pltpu.VMEM((TOKENS, HEAD), jnp.float32),
            pltpu.VMEM((PEERS, ROWS, HEAD), jnp.bfloat16),
            pltpu.VMEM((ROWS, wide), jnp.bfloat16),
            pltpu.VMEM((PEERS, ROWS), jnp.int32),
            pltpu.SMEM((PEERS, ROWS), jnp.int32),
            pltpu.SMEM((PEERS,), jnp.int32),
            *sems,
            pltpu.SemaphoreType.DMA((6,)),
        ],
        compiler_params=pltpu.CompilerParams(
            collective_id=0, has_side_effects=True, vmem_limit_bytes=60 * 1024 * 1024
        ),
        cost_estimate=pl.CostEstimate(
            flops=4 * pairs, bytes_accessed=6 * ROWS * wide * 2, transcendentals=TOKENS * TOKENS
        ),
        name="attend_and_exchange",
    )(planes, hidden[0], cells, frame_flags)
    return result[None]


def solution(mesh):
    in_specs = (
        P("grp", ("rep", "seq"), None, None),
        P("grp", ("rep", "seq"), None),
        P("rep"),
        P("rep"),
    )
    out_specs = P("grp", ("rep", "seq"), None)
    return jax.shard_map(local, mesh=mesh, in_specs=in_specs, out_specs=out_specs, check_vma=False)
```

```python
import math

import jax
import jax.numpy as jnp
from jax import lax
from jax.experimental import pallas as pl
from jax.experimental.pallas import tpu as pltpu
from jax.sharding import PartitionSpec as P

HEAD = 128
ROWS = 128
PEERS = 32
ZS = 8
YS = 4
TOKENS = ROWS * PEERS
FRAMES = 4
PAIR = 2
BLOCK = PAIR * ROWS
CHUNK = 512
LEAD = 4
HELD = 12
SCALE = HEAD ** -0.5 * math.log2(math.e)
MESH = pl.DeviceIdType.MESH
LAST_DIMS = (((1,), (1,)), ((), ()))


def offset(step):
    turn = lax.rem(step, ZS)
    dz = jnp.where(lax.rem(turn, 2) == 1, ZS - (turn + 1) // 2, turn // 2)
    return dz, step // ZS


def ahead(me, step):
    dz, dy = offset(step)
    return lax.rem(me // YS + dz, ZS) * YS + lax.rem(lax.rem(me, YS) + dy, YS)


def behind(me, step):
    dz, dy = offset(step)
    return lax.rem(me // YS + ZS - dz, ZS) * YS + lax.rem(lax.rem(me, YS) + YS - dy, YS)


def columns(peer):
    return pl.ds(pl.multiple_of(peer * HEAD, HEAD), HEAD)


def score(queries, keys, scores, peak):
    highest = jnp.full((BLOCK, 128), -jnp.inf, jnp.float32)
    for start in range(0, TOKENS, CHUNK):
        part = lax.dot_general(
            queries, keys[pl.ds(start, CHUNK), :], LAST_DIMS, preferred_element_type=jnp.float32
        )
        scores[:, pl.ds(start, CHUNK)] = part
        for lane in range(0, CHUNK, 128):
            highest = jnp.maximum(highest, part[:, lane:lane + 128])
    peak[...] = jnp.broadcast_to(jnp.max(highest, axis=1, keepdims=True), (BLOCK, 128))


def blend(values, scores, peak, queries=None, keys=None, next_scores=None):
    level = peak[...]
    totals = jnp.zeros((BLOCK, 128), jnp.float32)
    blended = jnp.zeros((BLOCK, HEAD), jnp.float32)
    highest = jnp.full((BLOCK, 128), -jnp.inf, jnp.float32)
    for start in range(0, TOKENS, CHUNK):
        if queries is not None:
            part = lax.dot_general(
                queries, keys[pl.ds(start, CHUNK), :], LAST_DIMS, preferred_element_type=jnp.float32
            )
        rounded = []
        for lane in range(0, CHUNK, 128):
            weights = jnp.exp2((scores[:, pl.ds(start + lane, 128)] - level) * SCALE)
            totals = totals + weights
            rounded.append(weights.astype(jnp.bfloat16))
        if queries is not None:
            next_scores[:, pl.ds(start, CHUNK)] = part
            for lane in range(0, CHUNK, 128):
                highest = jnp.maximum(highest, part[:, lane:lane + 128])
        blended = blended + jnp.dot(
            jnp.concatenate(rounded, axis=1),
            values[pl.ds(start, CHUNK), :],
            preferred_element_type=jnp.float32,
        )
    if queries is not None:
        peak[...] = jnp.broadcast_to(jnp.max(highest, axis=1, keepdims=True), (BLOCK, 128))
    return (blended / jnp.sum(totals, axis=1, keepdims=True)).astype(jnp.bfloat16)


def kernel(
    qkv, hidden, row_map, frame_flags, out,
    keys, values, queries, even, odd, peak, attended, ordered, hint, placed, landed, stream,
    flags, map_rows, map_cells, owner_of, slot_of,
    k_sent, k_got, v_sent, v_got, q_sent, q_got, back_sent, back_got, hint_sent, hint_got, out_sem, local_sem, turn,
):
    grp = lax.axis_index("grp")
    me = lax.axis_index("seq")

    def push(src, dst, sent, got, step, **device):
        return pltpu.make_async_remote_copy(
            src_ref=src, dst_ref=dst, send_sem=sent.at[step], recv_sem=got.at[step],
            device_id=device, device_id_type=MESH,
        )

    def key_copy(step):
        peer = ahead(me, step)
        return push(qkv.at[1, :, columns(peer)], keys.at[step], k_sent, k_got, step, seq=peer)

    def value_copy(step):
        peer = ahead(me, step)
        return push(qkv.at[2, :, columns(peer)], values.at[step], v_sent, v_got, step, seq=peer)

    def query_copy(step):
        peer = ahead(me, step)
        return push(qkv.at[0, :, columns(peer)], queries.at[step], q_sent, q_got, step, seq=peer)

    def back_copy(step):
        return push(attended.at[step], landed.at[step], back_sent, back_got, step, seq=behind(me, step))

    def hint_copy(step):
        return push(ordered.at[step], hint.at[step], hint_sent, hint_got, step, grp=1 - grp)

    def each(first, last, body):
        def step(i, carry):
            body(i)
            return carry
        lax.fori_loop(first, last, step, 0)

    own = [
        pltpu.make_async_copy(qkv.at[1, :, columns(me)], keys.at[0], local_sem.at[0]),
        pltpu.make_async_copy(qkv.at[2, :, columns(me)], values.at[0], local_sem.at[1]),
        pltpu.make_async_copy(qkv.at[0, :, columns(me)], queries.at[0], local_sem.at[2]),
        pltpu.make_async_copy(hidden, stream, local_sem.at[3]),
        pltpu.make_async_copy(row_map, map_rows, local_sem.at[4]),
        pltpu.make_async_copy(row_map, map_cells, local_sem.at[5]),
        pltpu.make_async_copy(frame_flags, flags, local_sem.at[6]),
    ]
    barrier = pltpu.get_barrier_semaphore()
    each(1, PEERS, lambda i: pl.semaphore_signal(
        barrier, inc=1, device_id={"seq": ahead(me, i)}, device_id_type=MESH))
    pl.semaphore_signal(barrier, inc=1, device_id={"grp": 1 - grp}, device_id_type=MESH)
    pl.semaphore_wait(barrier, PEERS)

    for copy in own:
        copy.start()

    def send_keys_values():
        each(1, PEERS, lambda i: key_copy(i).start())
        each(1, PEERS, lambda i: value_copy(i).start())

    @pl.when(grp == 0)
    def _():
        send_keys_values()

        def find(residue):
            def look(c, found):
                return jnp.where(lax.rem(map_cells[c, 0], PEERS) == residue, c, found)
            source = lax.fori_loop(0, PEERS, look, 0)
            dz = lax.rem(me // YS + ZS - source // YS, ZS)
            dy = lax.rem(lax.rem(me, YS) + YS - lax.rem(source, YS), YS)
            owner_of[residue] = source
            slot_of[residue] = dy * ZS + jnp.where(dz < ZS // 2, 2 * dz, 2 * ZS - 1 - 2 * dz)

        if LEAD:
            each(1, 1 + LEAD, lambda i: key_copy(i).wait_send())
            pl.semaphore_signal(turn, inc=1, device_id={"grp": 1}, device_id_type=MESH)
        own[5].wait()
        each(0, PEERS, find)
        each(1 + LEAD, PEERS, lambda i: key_copy(i).wait_send())

    @pl.when(grp == 1)
    def _():
        if LEAD:
            pl.semaphore_wait(turn, 1)
        send_keys_values()
        own[5].wait()
        each(1, PEERS, lambda i: key_copy(i).wait_send())

    each(1, PEERS, lambda i: value_copy(i).wait_send())
    each(1, PEERS, lambda i: query_copy(i).start())
    for copy in own[:5] + own[6:]:
        copy.wait()

    each(1, PEERS, lambda i: key_copy(i).wait_recv())
    each(1, PEERS, lambda i: value_copy(i).wait_recv())

    flat_keys = keys.reshape(TOKENS, HEAD)
    flat_values = values.reshape(TOKENS, HEAD)
    blocks = PEERS // PAIR

    def query_rows(block):
        for step in (block * PAIR, block * PAIR + 1):
            @pl.when(step > 0)
            def _():
                query_copy(step).wait_recv()
        return queries[pl.ds(block * PAIR, PAIR)].reshape(BLOCK, HEAD)

    def give_back(step):
        @pl.when(step > 0)
        def _():
            back_copy(step).start()

    def add_hint(step):
        token_peer = behind(me, step)
        hint_copy(step).wait_recv()
        gate = flags[token_peer // (PEERS // FRAMES)].astype(jnp.float32)
        total = attended[step].astype(jnp.float32) + gate * hint[step].astype(jnp.float32)
        attended[step] = total.astype(jnp.bfloat16)
        give_back(step)

    def deliver(block, result):
        first = block * PAIR
        attended[pl.ds(first, PAIR)] = result.reshape(PAIR, ROWS, HEAD)

        @pl.when(grp == 0)
        def _():
            for step in (first, first + 1):
                give_back(step)

        @pl.when(jnp.logical_and(grp == 1, block + 1 == HELD))
        def _():
            each(0, HELD * PAIR, add_hint)

        @pl.when(jnp.logical_and(grp == 1, block + 1 > HELD))
        def _():
            for step in (first, first + 1):
                add_hint(step)

    def work(block):
        rows = query_rows(block + 1)

        @pl.when(lax.rem(block, 2) == 0)
        def _():
            deliver(block, blend(flat_values, even, peak, rows, flat_keys, odd))

        @pl.when(lax.rem(block, 2) == 1)
        def _():
            deliver(block, blend(flat_values, odd, peak, rows, flat_keys, even))

    score(query_rows(0), flat_keys, even, peak)
    each(0, blocks - 1, work)
    deliver(blocks - 1, blend(flat_values, odd, peak))

    @pl.when(grp == 0)
    def _():
        def place(residue, carry):
            source = owner_of[residue]
            spots = map_rows[pl.ds(source, 1), :] // PEERS
            chosen = lax.broadcasted_iota(jnp.int32, (ROWS, ROWS), 0) == spots
            rows = jnp.dot(
                chosen.astype(jnp.bfloat16),
                attended[slot_of[residue]],
                preferred_element_type=jnp.float32,
            )
            placed[pl.ds(residue, ROWS, stride=PEERS), :] = rows
            return carry
        lax.fori_loop(0, PEERS, place, 0, unroll=8)

        def hand_over(step):
            token_peer = behind(me, step)
            rows = placed[pl.ds(pl.multiple_of(token_peer * ROWS, ROWS), ROWS), :]
            ordered[step] = rows.astype(jnp.bfloat16)
            hint_copy(step).start()
        each(0, PEERS, hand_over)

    each(1, PEERS, lambda i: query_copy(i).wait_send())

    def out_copy(step):
        cols = columns(ahead(me, step))
        return pltpu.make_async_copy(stream.at[:, cols], out.at[:, cols], out_sem.at[step])

    def finish(step, rows):
        cols = columns(ahead(me, step))
        total = stream[:, cols].astype(jnp.float32) + rows.astype(jnp.float32)
        out[:, cols] = total.astype(jnp.bfloat16)

    finish(0, attended[0])

    def finish_landed(step):
        back_copy(step).wait_recv()
        finish(step, landed[step])
    each(1, PEERS, finish_landed)

    each(1, PEERS, lambda i: back_copy(i).wait_send())

    @pl.when(grp == 0)
    def _():
        each(0, PEERS, lambda i: hint_copy(i).wait_send())


def local(qkv, hidden, row_map, frame_flags):
    planes = jnp.transpose(qkv[0], (1, 0, 2))
    cells = row_map.reshape(PEERS, ROWS)
    wide = PEERS * HEAD
    pairs = PEERS * TOKENS * HEAD * ROWS
    sems = [pltpu.SemaphoreType.DMA((PEERS,))] * 11
    result = pl.pallas_call(
        kernel,
        out_shape=pltpu.VMEM((ROWS, wide), jnp.bfloat16),
        in_specs=[
            pl.BlockSpec(memory_space=pl.ANY),
            pl.BlockSpec(memory_space=pl.ANY),
            pl.BlockSpec(memory_space=pl.ANY),
            pl.BlockSpec(memory_space=pl.ANY),
        ],
        out_specs=pl.BlockSpec(memory_space=pltpu.VMEM),
        scratch_shapes=[
            pltpu.VMEM((PEERS, ROWS, HEAD), jnp.bfloat16),
            pltpu.VMEM((PEERS, ROWS, HEAD), jnp.bfloat16),
            pltpu.VMEM((PEERS, ROWS, HEAD), jnp.bfloat16),
            pltpu.VMEM((BLOCK, TOKENS), jnp.float32),
            pltpu.VMEM((BLOCK, TOKENS), jnp.float32),
            pltpu.VMEM((BLOCK, 128), jnp.float32),
            pltpu.VMEM((PEERS, ROWS, HEAD), jnp.bfloat16),
            pltpu.VMEM((PEERS, ROWS, HEAD), jnp.bfloat16),
            pltpu.VMEM((PEERS, ROWS, HEAD), jnp.bfloat16),
            pltpu.VMEM((TOKENS, HEAD), jnp.float32),
            pltpu.VMEM((PEERS, ROWS, HEAD), jnp.bfloat16),
            pltpu.VMEM((ROWS, wide), jnp.bfloat16),
            pltpu.SMEM((FRAMES,), jnp.int32),
            pltpu.VMEM((PEERS, ROWS), jnp.int32),
            pltpu.SMEM((PEERS, ROWS), jnp.int32),
            pltpu.SMEM((PEERS,), jnp.int32),
            pltpu.SMEM((PEERS,), jnp.int32),
            *sems,
            pltpu.SemaphoreType.DMA((7,)),
            pltpu.SemaphoreType.REGULAR,
        ],
        compiler_params=pltpu.CompilerParams(
            collective_id=0, has_side_effects=True, vmem_limit_bytes=60 * 1024 * 1024
        ),
        cost_estimate=pl.CostEstimate(
            flops=4 * pairs, bytes_accessed=6 * ROWS * wide * 2, transcendentals=TOKENS * TOKENS
        ),
        name="attend_and_exchange",
    )(planes, hidden[0], cells, frame_flags)
    return result[None]


def solution(mesh):
    in_specs = (
        P("grp", ("rep", "seq"), None, None),
        P("grp", ("rep", "seq"), None),
        P("rep"),
        P("rep"),
    )
    out_specs = P("grp", ("rep", "seq"), None)
    return jax.shard_map(local, mesh=mesh, in_specs=in_specs, out_specs=out_specs, check_vma=False)
```

```python
import math

import jax
import jax.numpy as jnp
from jax import lax
from jax.experimental import pallas as pl
from jax.experimental.pallas import tpu as pltpu
from jax.sharding import PartitionSpec as P

HEAD = 128
ROWS = 128
PEERS = 32
ZS = 8
YS = 4
TOKENS = ROWS * PEERS
FRAMES = 4
PAIR = 2
BLOCK = PAIR * ROWS
CHUNK = 512
LEAD = 14
HELD = 10
LEAD_SENT, K_SENT, V_SENT, Q_SENT, BACK_SENT, HINT_SENT, K_GOT, V_GOT, HINT_GOT = range(9)
SCALE = HEAD ** -0.5 * math.log2(math.e)
MESH = pl.DeviceIdType.MESH
LAST_DIMS = (((1,), (1,)), ((), ()))


def offset(step):
    turn = lax.rem(step, ZS)
    dz = jnp.where(lax.rem(turn, 2) == 1, ZS - (turn + 1) // 2, turn // 2)
    return dz, step // ZS


def ahead(me, step):
    dz, dy = offset(step)
    return lax.rem(me // YS + dz, ZS) * YS + lax.rem(lax.rem(me, YS) + dy, YS)


def behind(me, step):
    dz, dy = offset(step)
    return lax.rem(me // YS + ZS - dz, ZS) * YS + lax.rem(lax.rem(me, YS) + YS - dy, YS)


def columns(peer):
    return pl.ds(pl.multiple_of(peer * HEAD, HEAD), HEAD)


def score(queries, keys, scores, peak):
    highest = jnp.full((BLOCK, 128), -jnp.inf, jnp.float32)
    for start in range(0, TOKENS, CHUNK):
        part = lax.dot_general(
            queries, keys[pl.ds(start, CHUNK), :], LAST_DIMS, preferred_element_type=jnp.float32
        )
        scores[:, pl.ds(start, CHUNK)] = part
        for lane in range(0, CHUNK, 128):
            highest = jnp.maximum(highest, part[:, lane:lane + 128])
    peak[...] = jnp.broadcast_to(jnp.max(highest, axis=1, keepdims=True), (BLOCK, 128))


def blend(values, scores, peak, queries=None, keys=None, next_scores=None):
    level = peak[...]
    totals = jnp.zeros((BLOCK, 128), jnp.float32)
    blended = jnp.zeros((BLOCK, HEAD), jnp.float32)
    highest = jnp.full((BLOCK, 128), -jnp.inf, jnp.float32)
    for start in range(0, TOKENS, CHUNK):
        if queries is not None:
            part = lax.dot_general(
                queries, keys[pl.ds(start, CHUNK), :], LAST_DIMS, preferred_element_type=jnp.float32
            )
        rounded = []
        for lane in range(0, CHUNK, 128):
            weights = jnp.exp2((scores[:, pl.ds(start + lane, 128)] - level) * SCALE)
            totals = totals + weights
            rounded.append(weights.astype(jnp.bfloat16))
        if queries is not None:
            next_scores[:, pl.ds(start, CHUNK)] = part
            for lane in range(0, CHUNK, 128):
                highest = jnp.maximum(highest, part[:, lane:lane + 128])
        blended = blended + jnp.dot(
            jnp.concatenate(rounded, axis=1),
            values[pl.ds(start, CHUNK), :],
            preferred_element_type=jnp.float32,
        )
    if queries is not None:
        peak[...] = jnp.broadcast_to(jnp.max(highest, axis=1, keepdims=True), (BLOCK, 128))
    return (blended / jnp.sum(totals, axis=1, keepdims=True)).astype(jnp.bfloat16)


def kernel(
    qkv, hidden, row_map, frame_flags, out,
    keys, values, queries, even, odd, peak, attended, ordered, hint, placed, landed, stream,
    flags, map_rows, map_cells, owner_of, slot_of,
    bulk, q_got, back_got, local_sem, turn,
):
    grp = lax.axis_index("grp")
    me = lax.axis_index("seq")

    def push(src, dst, sent, got, **device):
        return pltpu.make_async_remote_copy(
            src_ref=src, dst_ref=dst, send_sem=bulk.at[sent], recv_sem=got,
            device_id=device, device_id_type=MESH,
        )

    def key_copy(step, sent):
        peer = ahead(me, step)
        return push(qkv.at[1, :, columns(peer)], keys.at[step], sent, bulk.at[K_GOT], seq=peer)

    def value_copy(step):
        peer = ahead(me, step)
        return push(qkv.at[2, :, columns(peer)], values.at[step], V_SENT, bulk.at[V_GOT], seq=peer)

    def query_copy(step):
        peer = ahead(me, step)
        return push(
            qkv.at[0, :, columns(peer)], queries.at[step], Q_SENT, q_got.at[step // PAIR], seq=peer
        )

    def back_copy(step):
        return push(
            attended.at[step], landed.at[step], BACK_SENT, back_got.at[step // PAIR], seq=behind(me, step)
        )

    def hint_copy(step):
        return push(ordered.at[step], hint.at[step], HINT_SENT, bulk.at[HINT_GOT], grp=1 - grp)

    def whole(ref, first, count, sent, got):
        part = ref.at[pl.ds(first, count)]
        return push(part, part, sent, got, seq=ahead(me, 1))

    def each(first, last, body):
        def step(i, carry):
            body(i)
            return carry
        lax.fori_loop(first, last, step, 0)

    own = [
        pltpu.make_async_copy(qkv.at[1, :, columns(me)], keys.at[0], local_sem.at[0]),
        pltpu.make_async_copy(qkv.at[2, :, columns(me)], values.at[0], local_sem.at[1]),
        pltpu.make_async_copy(qkv.at[0, :, columns(me)], queries.at[0], local_sem.at[2]),
        pltpu.make_async_copy(hidden, stream, local_sem.at[3]),
        pltpu.make_async_copy(row_map, map_rows, local_sem.at[4]),
        pltpu.make_async_copy(row_map, map_cells, local_sem.at[5]),
        pltpu.make_async_copy(frame_flags, flags, local_sem.at[6]),
    ]
    barrier = pltpu.get_barrier_semaphore()
    each(1, PEERS, lambda i: pl.semaphore_signal(
        barrier, inc=1, device_id={"seq": ahead(me, i)}, device_id_type=MESH))
    pl.semaphore_signal(barrier, inc=1, device_id={"grp": 1 - grp}, device_id_type=MESH)
    pl.semaphore_wait(barrier, PEERS)

    for copy in own:
        copy.start()

    def send_keys_values():
        each(1, 1 + LEAD, lambda i: key_copy(i, LEAD_SENT).start())
        each(1 + LEAD, PEERS, lambda i: key_copy(i, K_SENT).start())
        each(1, PEERS, lambda i: value_copy(i).start())

    @pl.when(grp == 0)
    def _():
        send_keys_values()

        def find(residue):
            def look(c, found):
                return jnp.where(lax.rem(map_cells[c, 0], PEERS) == residue, c, found)
            source = lax.fori_loop(0, PEERS, look, 0)
            dz = lax.rem(me // YS + ZS - source // YS, ZS)
            dy = lax.rem(lax.rem(me, YS) + YS - lax.rem(source, YS), YS)
            owner_of[residue] = source
            slot_of[residue] = dy * ZS + jnp.where(dz < ZS // 2, 2 * dz, 2 * ZS - 1 - 2 * dz)

        whole(keys, 1, LEAD, LEAD_SENT, bulk.at[K_GOT]).wait_send()
        pl.semaphore_signal(turn, inc=1, device_id={"grp": 1}, device_id_type=MESH)
        own[5].wait()
        each(0, PEERS, find)

    @pl.when(grp == 1)
    def _():
        pl.semaphore_wait(turn, 1)
        send_keys_values()
        whole(keys, 1, LEAD, LEAD_SENT, bulk.at[K_GOT]).wait_send()
        own[5].wait()

    whole(keys, 1 + LEAD, PEERS - 1 - LEAD, K_SENT, bulk.at[K_GOT]).wait_send()
    whole(values, 1, PEERS - 1, V_SENT, bulk.at[V_GOT]).wait_send()
    each(1, PEERS, lambda i: query_copy(i).start())
    for copy in own[:5] + own[6:]:
        copy.wait()
    whole(keys, 1, PEERS - 1, K_SENT, bulk.at[K_GOT]).wait_recv()
    whole(values, 1, PEERS - 1, V_SENT, bulk.at[V_GOT]).wait_recv()

    flat_keys = keys.reshape(TOKENS, HEAD)
    flat_values = values.reshape(TOKENS, HEAD)
    blocks = PEERS // PAIR

    def query_rows(block):
        whole(queries, block * PAIR, PAIR, Q_SENT, q_got.at[block]).wait_recv()
        return queries[pl.ds(block * PAIR, PAIR)].reshape(BLOCK, HEAD)

    def give_back(step):
        @pl.when(step > 0)
        def _():
            back_copy(step).start()

    def add_hint(step):
        token_peer = behind(me, step)
        gate = flags[token_peer // (PEERS // FRAMES)].astype(jnp.float32)
        total = attended[step].astype(jnp.float32) + gate * hint[step].astype(jnp.float32)
        attended[step] = total.astype(jnp.bfloat16)
        give_back(step)

    def deliver(block, result):
        first = block * PAIR
        attended[pl.ds(first, PAIR)] = result.reshape(PAIR, ROWS, HEAD)

        @pl.when(grp == 0)
        def _():
            for step in (first, first + 1):
                give_back(step)

        @pl.when(jnp.logical_and(grp == 1, block + 1 == HELD))
        def _():
            whole(hint, 0, PEERS, HINT_SENT, bulk.at[HINT_GOT]).wait_recv()
            each(0, HELD * PAIR, add_hint)

        @pl.when(jnp.logical_and(grp == 1, block + 1 > HELD))
        def _():
            for step in (first, first + 1):
                add_hint(step)

    def work(block):
        rows = query_rows(block + 1)

        @pl.when(lax.rem(block, 2) == 0)
        def _():
            deliver(block, blend(flat_values, even, peak, rows, flat_keys, odd))

        @pl.when(lax.rem(block, 2) == 1)
        def _():
            deliver(block, blend(flat_values, odd, peak, rows, flat_keys, even))

    whole(queries, 1, PAIR - 1, Q_SENT, q_got.at[0]).wait_recv()
    score(queries[pl.ds(0, PAIR)].reshape(BLOCK, HEAD), flat_keys, even, peak)
    each(0, blocks - 1, work)
    deliver(blocks - 1, blend(flat_values, odd, peak))

    @pl.when(grp == 0)
    def _():
        def place(residue, carry):
            source = owner_of[residue]
            spots = map_rows[pl.ds(source, 1), :] // PEERS
            chosen = lax.broadcasted_iota(jnp.int32, (ROWS, ROWS), 0) == spots
            rows = jnp.dot(
                chosen.astype(jnp.bfloat16),
                attended[slot_of[residue]],
                preferred_element_type=jnp.float32,
            )
            placed[pl.ds(residue, ROWS, stride=PEERS), :] = rows
            return carry
        lax.fori_loop(0, PEERS, place, 0, unroll=8)

        def hand_over(step):
            token_peer = behind(me, step)
            rows = placed[pl.ds(pl.multiple_of(token_peer * ROWS, ROWS), ROWS), :]
            ordered[step] = rows.astype(jnp.bfloat16)
            hint_copy(step).start()
        each(0, PEERS, hand_over)

    whole(queries, 1, PEERS - 1, Q_SENT, q_got.at[0]).wait_send()

    def finish(step, rows):
        cols = columns(ahead(me, step))
        total = stream[:, cols].astype(jnp.float32) + rows.astype(jnp.float32)
        out[:, cols] = total.astype(jnp.bfloat16)

    finish(0, attended[0])
    whole(landed, 1, PAIR - 1, BACK_SENT, back_got.at[0]).wait_recv()
    each(1, PAIR, lambda i: finish(i, landed[i]))

    def finish_block(block):
        whole(landed, block * PAIR, PAIR, BACK_SENT, back_got.at[block]).wait_recv()
        for step in (block * PAIR, block * PAIR + 1):
            finish(step, landed[step])
    each(1, blocks, finish_block)

    whole(attended, 1, PEERS - 1, BACK_SENT, back_got.at[0]).wait_send()

    @pl.when(grp == 0)
    def _():
        whole(ordered, 0, PEERS, HINT_SENT, bulk.at[HINT_GOT]).wait_send()


def local(qkv, hidden, row_map, frame_flags):
    planes = jnp.transpose(qkv[0], (1, 0, 2))
    cells = row_map.reshape(PEERS, ROWS)
    wide = PEERS * HEAD
    pairs = PEERS * TOKENS * HEAD * ROWS
    result = pl.pallas_call(
        kernel,
        out_shape=pltpu.VMEM((ROWS, wide), jnp.bfloat16),
        in_specs=[
            pl.BlockSpec(memory_space=pl.ANY),
            pl.BlockSpec(memory_space=pl.ANY),
            pl.BlockSpec(memory_space=pl.ANY),
            pl.BlockSpec(memory_space=pl.ANY),
        ],
        out_specs=pl.BlockSpec(memory_space=pltpu.VMEM),
        scratch_shapes=[
            pltpu.VMEM((PEERS, ROWS, HEAD), jnp.bfloat16),
            pltpu.VMEM((PEERS, ROWS, HEAD), jnp.bfloat16),
            pltpu.VMEM((PEERS, ROWS, HEAD), jnp.bfloat16),
            pltpu.VMEM((BLOCK, TOKENS), jnp.float32),
            pltpu.VMEM((BLOCK, TOKENS), jnp.float32),
            pltpu.VMEM((BLOCK, 128), jnp.float32),
            pltpu.VMEM((PEERS, ROWS, HEAD), jnp.bfloat16),
            pltpu.VMEM((PEERS, ROWS, HEAD), jnp.bfloat16),
            pltpu.VMEM((PEERS, ROWS, HEAD), jnp.bfloat16),
            pltpu.VMEM((TOKENS, HEAD), jnp.float32),
            pltpu.VMEM((PEERS, ROWS, HEAD), jnp.bfloat16),
            pltpu.VMEM((ROWS, wide), jnp.bfloat16),
            pltpu.SMEM((FRAMES,), jnp.int32),
            pltpu.VMEM((PEERS, ROWS), jnp.int32),
            pltpu.SMEM((PEERS, ROWS), jnp.int32),
            pltpu.SMEM((PEERS,), jnp.int32),
            pltpu.SMEM((PEERS,), jnp.int32),
            pltpu.SemaphoreType.DMA((9,)),
            pltpu.SemaphoreType.DMA((PEERS // PAIR,)),
            pltpu.SemaphoreType.DMA((PEERS // PAIR,)),
            pltpu.SemaphoreType.DMA((7,)),
            pltpu.SemaphoreType.REGULAR,
        ],
        compiler_params=pltpu.CompilerParams(
            collective_id=0, has_side_effects=True, vmem_limit_bytes=60 * 1024 * 1024
        ),
        cost_estimate=pl.CostEstimate(
            flops=4 * pairs, bytes_accessed=6 * ROWS * wide * 2, transcendentals=TOKENS * TOKENS
        ),
        name="attend_and_exchange",
    )(planes, hidden[0], cells, frame_flags)
    return result[None]


def solution(mesh):
    in_specs = (
        P("grp", ("rep", "seq"), None, None),
        P("grp", ("rep", "seq"), None),
        P("rep"),
        P("rep"),
    )
    out_specs = P("grp", ("rep", "seq"), None)
    return jax.shard_map(local, mesh=mesh, in_specs=in_specs, out_specs=out_specs, check_vma=False)
```

```python
import math

import jax
import jax.numpy as jnp
from jax import lax
from jax.experimental import pallas as pl
from jax.experimental.pallas import tpu as pltpu
from jax.sharding import PartitionSpec as P

HEAD = 128
ROWS = 128
PEERS = 32
ZS = 8
YS = 4
TOKENS = ROWS * PEERS
FRAMES = 4
PAIR = 2
BLOCK = PAIR * ROWS
CHUNK = 512
LEAD = 14
HELD = 10
LEAD_SENT, K_SENT, V_SENT, Q_SENT, BACK_SENT, HINT_SENT, K_GOT, V_GOT, HINT_GOT = range(9)
SCALE = HEAD ** -0.5 * math.log2(math.e)
MESH = pl.DeviceIdType.MESH
LAST_DIMS = (((1,), (1,)), ((), ()))


def offset(step):
    turn = lax.rem(step, ZS)
    dz = jnp.where(lax.rem(turn, 2) == 1, ZS - (turn + 1) // 2, turn // 2)
    return dz, step // ZS


def ahead(me, step):
    dz, dy = offset(step)
    return lax.rem(me // YS + dz, ZS) * YS + lax.rem(lax.rem(me, YS) + dy, YS)


def behind(me, step):
    dz, dy = offset(step)
    return lax.rem(me // YS + ZS - dz, ZS) * YS + lax.rem(lax.rem(me, YS) + YS - dy, YS)


def columns(peer):
    return pl.ds(pl.multiple_of(peer * HEAD, HEAD), HEAD)


def score(queries, keys, scores, peak):
    highest = jnp.full((BLOCK, 128), -jnp.inf, jnp.float32)
    for start in range(0, TOKENS, CHUNK):
        part = lax.dot_general(
            queries, keys[pl.ds(start, CHUNK), :], LAST_DIMS, preferred_element_type=jnp.float32
        )
        scores[:, pl.ds(start, CHUNK)] = part
        for lane in range(0, CHUNK, 128):
            highest = jnp.maximum(highest, part[:, lane:lane + 128])
    peak[...] = jnp.broadcast_to(jnp.max(highest, axis=1, keepdims=True), (BLOCK, 128))


def blend(values, scores, peak, queries=None, keys=None, next_scores=None):
    level = peak[...]
    totals = jnp.zeros((BLOCK, 128), jnp.float32)
    blended = jnp.zeros((BLOCK, HEAD), jnp.float32)
    highest = jnp.full((BLOCK, 128), -jnp.inf, jnp.float32)
    for start in range(0, TOKENS, CHUNK):
        if queries is not None:
            part = lax.dot_general(
                queries, keys[pl.ds(start, CHUNK), :], LAST_DIMS, preferred_element_type=jnp.float32
            )
        rounded = []
        for lane in range(0, CHUNK, 128):
            weights = jnp.exp2((scores[:, pl.ds(start + lane, 128)] - level) * SCALE)
            totals = totals + weights
            rounded.append(weights.astype(jnp.bfloat16))
        if queries is not None:
            next_scores[:, pl.ds(start, CHUNK)] = part
            for lane in range(0, CHUNK, 128):
                highest = jnp.maximum(highest, part[:, lane:lane + 128])
        blended = blended + jnp.dot(
            jnp.concatenate(rounded, axis=1),
            values[pl.ds(start, CHUNK), :],
            preferred_element_type=jnp.float32,
        )
    if queries is not None:
        peak[...] = jnp.broadcast_to(jnp.max(highest, axis=1, keepdims=True), (BLOCK, 128))
    return (blended / jnp.sum(totals, axis=1, keepdims=True)).astype(jnp.bfloat16)


def kernel(
    qkv, hidden, row_map, frame_flags, out,
    keys, values, queries, even, odd, peak, attended, ordered, hint, placed, landed, stream,
    flags, map_rows, map_cells, owner_of, slot_of,
    bulk, q_got, back_got, local_sem, turn,
):
    grp = lax.axis_index("grp")
    me = lax.axis_index("seq")

    def push(src, dst, sent, got, **device):
        return pltpu.make_async_remote_copy(
            src_ref=src, dst_ref=dst, send_sem=bulk.at[sent], recv_sem=got,
            device_id=device, device_id_type=MESH,
        )

    def key_copy(step, sent):
        peer = ahead(me, step)
        return push(qkv.at[1, :, columns(peer)], keys.at[step], sent, bulk.at[K_GOT], seq=peer)

    def value_copy(step):
        peer = ahead(me, step)
        return push(qkv.at[2, :, columns(peer)], values.at[step], V_SENT, bulk.at[V_GOT], seq=peer)

    def query_copy(step):
        peer = ahead(me, step)
        return push(
            qkv.at[0, :, columns(peer)], queries.at[step], Q_SENT, q_got.at[step // PAIR], seq=peer
        )

    def back_copy(step):
        return push(
            attended.at[step], landed.at[step], BACK_SENT, back_got.at[step // PAIR], seq=behind(me, step)
        )

    def hint_copy(step):
        return push(ordered.at[step], hint.at[step], HINT_SENT, bulk.at[HINT_GOT], grp=1 - grp)

    def whole(ref, first, count, sent, got):
        part = ref.at[pl.ds(first, count)]
        return push(part, part, sent, got, seq=ahead(me, 1))

    def each(first, last, body):
        def step(i, carry):
            body(i)
            return carry
        lax.fori_loop(first, last, step, 0)

    own = [
        pltpu.make_async_copy(qkv.at[1, :, columns(me)], keys.at[0], local_sem.at[0]),
        pltpu.make_async_copy(qkv.at[2, :, columns(me)], values.at[0], local_sem.at[1]),
        pltpu.make_async_copy(qkv.at[0, :, columns(me)], queries.at[0], local_sem.at[2]),
        pltpu.make_async_copy(hidden, stream, local_sem.at[3]),
        pltpu.make_async_copy(row_map, map_rows, local_sem.at[4]),
        pltpu.make_async_copy(row_map, map_cells, local_sem.at[5]),
        pltpu.make_async_copy(frame_flags, flags, local_sem.at[6]),
    ]
    barrier = pltpu.get_barrier_semaphore()
    each(1, PEERS, lambda i: pl.semaphore_signal(
        barrier, inc=1, device_id={"seq": ahead(me, i)}, device_id_type=MESH))
    pl.semaphore_signal(barrier, inc=1, device_id={"grp": 1 - grp}, device_id_type=MESH)
    pl.semaphore_wait(barrier, PEERS)

    def send_keys_values():
        each(1, 1 + LEAD, lambda i: key_copy(i, LEAD_SENT).start())
        each(1 + LEAD, PEERS, lambda i: key_copy(i, K_SENT).start())
        each(1, PEERS, lambda i: value_copy(i).start())

    @pl.when(grp == 0)
    def _():
        send_keys_values()
        for copy in own:
            copy.start()

        def find(residue):
            def look(c, found):
                return jnp.where(lax.rem(map_cells[c, 0], PEERS) == residue, c, found)
            source = lax.fori_loop(0, PEERS, look, 0)
            dz = lax.rem(me // YS + ZS - source // YS, ZS)
            dy = lax.rem(lax.rem(me, YS) + YS - lax.rem(source, YS), YS)
            owner_of[residue] = source
            slot_of[residue] = dy * ZS + jnp.where(dz < ZS // 2, 2 * dz, 2 * ZS - 1 - 2 * dz)

        whole(keys, 1, LEAD, LEAD_SENT, bulk.at[K_GOT]).wait_send()
        pl.semaphore_signal(turn, inc=1, device_id={"grp": 1}, device_id_type=MESH)
        own[5].wait()
        each(0, PEERS, find)

    @pl.when(grp == 1)
    def _():
        for copy in own:
            copy.start()
        pl.semaphore_wait(turn, 1)
        send_keys_values()
        whole(keys, 1, LEAD, LEAD_SENT, bulk.at[K_GOT]).wait_send()
        own[5].wait()

    whole(keys, 1 + LEAD, PEERS - 1 - LEAD, K_SENT, bulk.at[K_GOT]).wait_send()
    whole(values, 1, PEERS - 1, V_SENT, bulk.at[V_GOT]).wait_send()
    each(1, PEERS, lambda i: query_copy(i).start())
    for copy in own[:5] + own[6:]:
        copy.wait()
    whole(keys, 1, PEERS - 1, K_SENT, bulk.at[K_GOT]).wait_recv()
    whole(values, 1, PEERS - 1, V_SENT, bulk.at[V_GOT]).wait_recv()

    flat_keys = keys.reshape(TOKENS, HEAD)
    flat_values = values.reshape(TOKENS, HEAD)
    blocks = PEERS // PAIR

    def query_rows(block):
        whole(queries, block * PAIR, PAIR, Q_SENT, q_got.at[block]).wait_recv()
        return queries[pl.ds(block * PAIR, PAIR)].reshape(BLOCK, HEAD)

    def give_back(step):
        @pl.when(step > 0)
        def _():
            back_copy(step).start()

    def add_hint(step):
        token_peer = behind(me, step)
        gate = flags[token_peer // (PEERS // FRAMES)].astype(jnp.float32)
        total = attended[step].astype(jnp.float32) + gate * hint[step].astype(jnp.float32)
        attended[step] = total.astype(jnp.bfloat16)
        give_back(step)

    def deliver(block, result):
        first = block * PAIR
        attended[pl.ds(first, PAIR)] = result.reshape(PAIR, ROWS, HEAD)

        @pl.when(grp == 0)
        def _():
            for step in (first, first + 1):
                give_back(step)

        @pl.when(jnp.logical_and(grp == 1, block + 1 == HELD))
        def _():
            whole(hint, 0, PEERS, HINT_SENT, bulk.at[HINT_GOT]).wait_recv()
            each(0, HELD * PAIR, add_hint)

        @pl.when(jnp.logical_and(grp == 1, block + 1 > HELD))
        def _():
            for step in (first, first + 1):
                add_hint(step)

    def work(block):
        rows = query_rows(block + 1)

        @pl.when(lax.rem(block, 2) == 0)
        def _():
            deliver(block, blend(flat_values, even, peak, rows, flat_keys, odd))

        @pl.when(lax.rem(block, 2) == 1)
        def _():
            deliver(block, blend(flat_values, odd, peak, rows, flat_keys, even))

    whole(queries, 1, PAIR - 1, Q_SENT, q_got.at[0]).wait_recv()
    score(queries[pl.ds(0, PAIR)].reshape(BLOCK, HEAD), flat_keys, even, peak)
    each(0, blocks - 1, work)
    deliver(blocks - 1, blend(flat_values, odd, peak))

    @pl.when(grp == 0)
    def _():
        def place(residue, carry):
            source = owner_of[residue]
            spots = map_rows[pl.ds(source, 1), :] // PEERS
            chosen = lax.broadcasted_iota(jnp.int32, (ROWS, ROWS), 0) == spots
            rows = jnp.dot(
                chosen.astype(jnp.bfloat16),
                attended[slot_of[residue]],
                preferred_element_type=jnp.float32,
            )
            placed[pl.ds(residue, ROWS, stride=PEERS), :] = rows
            return carry
        lax.fori_loop(0, PEERS, place, 0, unroll=8)

        def hand_over(step):
            token_peer = behind(me, step)
            rows = placed[pl.ds(pl.multiple_of(token_peer * ROWS, ROWS), ROWS), :]
            ordered[step] = rows.astype(jnp.bfloat16)
            hint_copy(step).start()
        each(0, PEERS, hand_over)

    whole(queries, 1, PEERS - 1, Q_SENT, q_got.at[0]).wait_send()

    def finish(step, rows):
        cols = columns(ahead(me, step))
        total = stream[:, cols].astype(jnp.float32) + rows.astype(jnp.float32)
        out[:, cols] = total.astype(jnp.bfloat16)

    finish(0, attended[0])
    whole(landed, 1, PAIR - 1, BACK_SENT, back_got.at[0]).wait_recv()
    each(1, PAIR, lambda i: finish(i, landed[i]))

    def finish_block(block):
        whole(landed, block * PAIR, PAIR, BACK_SENT, back_got.at[block]).wait_recv()
        for step in (block * PAIR, block * PAIR + 1):
            finish(step, landed[step])
    each(1, blocks, finish_block)

    whole(attended, 1, PEERS - 1, BACK_SENT, back_got.at[0]).wait_send()

    @pl.when(grp == 0)
    def _():
        whole(ordered, 0, PEERS, HINT_SENT, bulk.at[HINT_GOT]).wait_send()


def local(qkv, hidden, row_map, frame_flags):
    planes = jnp.transpose(qkv[0], (1, 0, 2))
    cells = row_map.reshape(PEERS, ROWS)
    wide = PEERS * HEAD
    pairs = PEERS * TOKENS * HEAD * ROWS
    result = pl.pallas_call(
        kernel,
        out_shape=pltpu.VMEM((ROWS, wide), jnp.bfloat16),
        in_specs=[
            pl.BlockSpec(memory_space=pl.ANY),
            pl.BlockSpec(memory_space=pl.ANY),
            pl.BlockSpec(memory_space=pl.ANY),
            pl.BlockSpec(memory_space=pl.ANY),
        ],
        out_specs=pl.BlockSpec(memory_space=pltpu.VMEM),
        scratch_shapes=[
            pltpu.VMEM((PEERS, ROWS, HEAD), jnp.bfloat16),
            pltpu.VMEM((PEERS, ROWS, HEAD), jnp.bfloat16),
            pltpu.VMEM((PEERS, ROWS, HEAD), jnp.bfloat16),
            pltpu.VMEM((BLOCK, TOKENS), jnp.float32),
            pltpu.VMEM((BLOCK, TOKENS), jnp.float32),
            pltpu.VMEM((BLOCK, 128), jnp.float32),
            pltpu.VMEM((PEERS, ROWS, HEAD), jnp.bfloat16),
            pltpu.VMEM((PEERS, ROWS, HEAD), jnp.bfloat16),
            pltpu.VMEM((PEERS, ROWS, HEAD), jnp.bfloat16),
            pltpu.VMEM((TOKENS + PEERS, HEAD), jnp.float32),
            pltpu.VMEM((PEERS, ROWS, HEAD), jnp.bfloat16),
            pltpu.VMEM((ROWS, wide), jnp.bfloat16),
            pltpu.SMEM((FRAMES,), jnp.int32),
            pltpu.VMEM((PEERS, ROWS), jnp.int32),
            pltpu.SMEM((PEERS, ROWS), jnp.int32),
            pltpu.SMEM((PEERS,), jnp.int32),
            pltpu.SMEM((PEERS,), jnp.int32),
            pltpu.SemaphoreType.DMA((9,)),
            pltpu.SemaphoreType.DMA((PEERS // PAIR,)),
            pltpu.SemaphoreType.DMA((PEERS // PAIR,)),
            pltpu.SemaphoreType.DMA((7,)),
            pltpu.SemaphoreType.REGULAR,
        ],
        compiler_params=pltpu.CompilerParams(
            collective_id=0, has_side_effects=True, vmem_limit_bytes=60 * 1024 * 1024
        ),
        cost_estimate=pl.CostEstimate(
            flops=4 * pairs, bytes_accessed=6 * ROWS * wide * 2, transcendentals=TOKENS * TOKENS
        ),
        name="attend_and_exchange",
    )(planes, hidden[0], cells, frame_flags)
    return result[None]


def solution(mesh):
    in_specs = (
        P("grp", ("rep", "seq"), None, None),
        P("grp", ("rep", "seq"), None),
        P("rep"),
        P("rep"),
    )
    out_specs = P("grp", ("rep", "seq"), None)
    return jax.shard_map(local, mesh=mesh, in_specs=in_specs, out_specs=out_specs, check_vma=False)
```

```python
import math

import jax
import jax.numpy as jnp
from jax import lax
from jax.experimental import pallas as pl
from jax.experimental.pallas import tpu as pltpu
from jax.sharding import PartitionSpec as P

HEAD = 128
ROWS = 128
PEERS = 32
ZS = 8
YS = 4
TOKENS = ROWS * PEERS
FRAMES = 4
PAIR = 2
BLOCK = PAIR * ROWS
CHUNK = 512
LEAD = 14
HELD = 10
LEAD_SENT, K_SENT, V_SENT, Q_SENT, BACK_SENT, HINT_SENT, K_GOT, V_GOT, HINT_GOT = range(9)
SCALE = HEAD ** -0.5 * math.log2(math.e)
MESH = pl.DeviceIdType.MESH
LAST_DIMS = (((1,), (1,)), ((), ()))


def offset(step):
    turn = lax.rem(step, ZS)
    dz = jnp.where(lax.rem(turn, 2) == 1, ZS - (turn + 1) // 2, turn // 2)
    return dz, step // ZS


def ahead(me, step):
    dz, dy = offset(step)
    return lax.rem(me // YS + dz, ZS) * YS + lax.rem(lax.rem(me, YS) + dy, YS)


def behind(me, step):
    dz, dy = offset(step)
    return lax.rem(me // YS + ZS - dz, ZS) * YS + lax.rem(lax.rem(me, YS) + YS - dy, YS)


def columns(peer):
    return pl.ds(pl.multiple_of(peer * HEAD, HEAD), HEAD)


def score(queries, keys, scores, peak):
    highest = jnp.full((BLOCK, 128), -jnp.inf, jnp.float32)
    for start in range(0, TOKENS, CHUNK):
        part = lax.dot_general(
            queries, keys[pl.ds(start, CHUNK), :], LAST_DIMS, preferred_element_type=jnp.float32
        )
        scores[:, pl.ds(start, CHUNK)] = part
        for lane in range(0, CHUNK, 128):
            highest = jnp.maximum(highest, part[:, lane:lane + 128])
    peak[...] = jnp.broadcast_to(jnp.max(highest, axis=1, keepdims=True), (BLOCK, 128))


def blend(values, scores, peak, queries=None, keys=None, next_scores=None):
    level = peak[...]
    totals = jnp.zeros((BLOCK, 128), jnp.float32)
    blended = jnp.zeros((BLOCK, HEAD), jnp.float32)
    highest = jnp.full((BLOCK, 128), -jnp.inf, jnp.float32)
    for start in range(0, TOKENS, CHUNK):
        if queries is not None:
            part = lax.dot_general(
                queries, keys[pl.ds(start, CHUNK), :], LAST_DIMS, preferred_element_type=jnp.float32
            )
        rounded = []
        for lane in range(0, CHUNK, 128):
            weights = jnp.exp2((scores[:, pl.ds(start + lane, 128)] - level) * SCALE)
            totals = totals + weights
            rounded.append(weights.astype(jnp.bfloat16))
        if queries is not None:
            next_scores[:, pl.ds(start, CHUNK)] = part
            for lane in range(0, CHUNK, 128):
                highest = jnp.maximum(highest, part[:, lane:lane + 128])
        blended = blended + jnp.dot(
            jnp.concatenate(rounded, axis=1),
            values[pl.ds(start, CHUNK), :],
            preferred_element_type=jnp.float32,
        )
    if queries is not None:
        peak[...] = jnp.broadcast_to(jnp.max(highest, axis=1, keepdims=True), (BLOCK, 128))
    return (blended / jnp.sum(totals, axis=1, keepdims=True)).astype(jnp.bfloat16)


def kernel(
    qkv, hidden, row_map, frame_flags, out,
    keys, values, queries, even, odd, peak, attended, ordered, hint, placed, landed, stream,
    flags, map_rows, map_cells, owner_of, slot_of,
    bulk, q_got, back_got, local_sem, turn,
):
    grp = lax.axis_index("grp")
    me = lax.axis_index("seq")

    def push(src, dst, sent, got, **device):
        return pltpu.make_async_remote_copy(
            src_ref=src, dst_ref=dst, send_sem=bulk.at[sent], recv_sem=got,
            device_id=device, device_id_type=MESH,
        )

    def key_copy(step, sent):
        peer = ahead(me, step)
        return push(qkv.at[1, :, columns(peer)], keys.at[step], sent, bulk.at[K_GOT], seq=peer)

    def value_copy(step):
        peer = ahead(me, step)
        return push(qkv.at[2, :, columns(peer)], values.at[step], V_SENT, bulk.at[V_GOT], seq=peer)

    def query_copy(step):
        peer = ahead(me, step)
        return push(
            qkv.at[0, :, columns(peer)], queries.at[step], Q_SENT, q_got.at[step // PAIR], seq=peer
        )

    def back_copy(step):
        return push(
            attended.at[step], landed.at[step], BACK_SENT, back_got.at[step // PAIR], seq=behind(me, step)
        )

    def hint_copy(step):
        return push(ordered.at[step], hint.at[step], HINT_SENT, bulk.at[HINT_GOT], grp=1 - grp)

    def whole(ref, first, count, sent, got):
        part = ref.at[pl.ds(first, count)]
        return push(part, part, sent, got, seq=ahead(me, 1))

    def each(first, last, body, unroll=1):
        def step(i, carry):
            body(i)
            return carry
        lax.fori_loop(first, last, step, 0, unroll=unroll)

    own = [
        pltpu.make_async_copy(qkv.at[1, :, columns(me)], keys.at[0], local_sem.at[0]),
        pltpu.make_async_copy(qkv.at[2, :, columns(me)], values.at[0], local_sem.at[1]),
        pltpu.make_async_copy(qkv.at[0, :, columns(me)], queries.at[0], local_sem.at[2]),
        pltpu.make_async_copy(hidden, stream, local_sem.at[3]),
        pltpu.make_async_copy(row_map, map_rows, local_sem.at[4]),
        pltpu.make_async_copy(row_map, map_cells, local_sem.at[5]),
        pltpu.make_async_copy(frame_flags, flags, local_sem.at[6]),
    ]
    barrier = pltpu.get_barrier_semaphore()
    each(1, PEERS, lambda i: pl.semaphore_signal(
        barrier, inc=1, device_id={"seq": ahead(me, i)}, device_id_type=MESH), unroll=8)
    pl.semaphore_signal(barrier, inc=1, device_id={"grp": 1 - grp}, device_id_type=MESH)
    pl.semaphore_wait(barrier, PEERS)

    def send_keys_values():
        each(1, 1 + LEAD, lambda i: key_copy(i, LEAD_SENT).start(), unroll=7)
        each(1 + LEAD, PEERS, lambda i: key_copy(i, K_SENT).start(), unroll=8)
        each(1, PEERS, lambda i: value_copy(i).start(), unroll=8)

    @pl.when(grp == 0)
    def _():
        send_keys_values()
        for copy in own:
            copy.start()

        def find(residue):
            def look(c, found):
                return jnp.where(lax.rem(map_cells[c, 0], PEERS) == residue, c, found)
            source = lax.fori_loop(0, PEERS, look, 0)
            dz = lax.rem(me // YS + ZS - source // YS, ZS)
            dy = lax.rem(lax.rem(me, YS) + YS - lax.rem(source, YS), YS)
            owner_of[residue] = source
            slot_of[residue] = dy * ZS + jnp.where(dz < ZS // 2, 2 * dz, 2 * ZS - 1 - 2 * dz)

        whole(keys, 1, LEAD, LEAD_SENT, bulk.at[K_GOT]).wait_send()
        pl.semaphore_signal(turn, inc=1, device_id={"grp": 1}, device_id_type=MESH)
        own[5].wait()
        each(0, PEERS, find)

    @pl.when(grp == 1)
    def _():
        for copy in own:
            copy.start()
        pl.semaphore_wait(turn, 1)
        send_keys_values()
        whole(keys, 1, LEAD, LEAD_SENT, bulk.at[K_GOT]).wait_send()
        own[5].wait()

    whole(keys, 1 + LEAD, PEERS - 1 - LEAD, K_SENT, bulk.at[K_GOT]).wait_send()
    whole(values, 1, PEERS - 1, V_SENT, bulk.at[V_GOT]).wait_send()
    each(1, PEERS, lambda i: query_copy(i).start(), unroll=8)
    for copy in own[:5] + own[6:]:
        copy.wait()
    whole(keys, 1, PEERS - 1, K_SENT, bulk.at[K_GOT]).wait_recv()
    whole(values, 1, PEERS - 1, V_SENT, bulk.at[V_GOT]).wait_recv()

    flat_keys = keys.reshape(TOKENS, HEAD)
    flat_values = values.reshape(TOKENS, HEAD)
    blocks = PEERS // PAIR

    def query_rows(block):
        whole(queries, block * PAIR, PAIR, Q_SENT, q_got.at[block]).wait_recv()
        return queries[pl.ds(block * PAIR, PAIR)].reshape(BLOCK, HEAD)

    def give_back(step):
        @pl.when(step > 0)
        def _():
            back_copy(step).start()

    def add_hint(step):
        token_peer = behind(me, step)
        gate = flags[token_peer // (PEERS // FRAMES)].astype(jnp.float32)
        total = attended[step].astype(jnp.float32) + gate * hint[step].astype(jnp.float32)
        attended[step] = total.astype(jnp.bfloat16)
        give_back(step)

    def deliver(block, result):
        first = block * PAIR
        attended[pl.ds(first, PAIR)] = result.reshape(PAIR, ROWS, HEAD)

        @pl.when(grp == 0)
        def _():
            for step in (first, first + 1):
                give_back(step)

        @pl.when(jnp.logical_and(grp == 1, block + 1 == HELD))
        def _():
            whole(hint, 0, PEERS, HINT_SENT, bulk.at[HINT_GOT]).wait_recv()
            each(0, HELD * PAIR, add_hint, unroll=4)

        @pl.when(jnp.logical_and(grp == 1, block + 1 > HELD))
        def _():
            for step in (first, first + 1):
                add_hint(step)

    def work(block):
        rows = query_rows(block + 1)

        @pl.when(lax.rem(block, 2) == 0)
        def _():
            deliver(block, blend(flat_values, even, peak, rows, flat_keys, odd))

        @pl.when(lax.rem(block, 2) == 1)
        def _():
            deliver(block, blend(flat_values, odd, peak, rows, flat_keys, even))

    whole(queries, 1, PAIR - 1, Q_SENT, q_got.at[0]).wait_recv()
    score(queries[pl.ds(0, PAIR)].reshape(BLOCK, HEAD), flat_keys, even, peak)
    each(0, blocks - 1, work)
    deliver(blocks - 1, blend(flat_values, odd, peak))

    @pl.when(grp == 0)
    def _():
        def place(residue, carry):
            source = owner_of[residue]
            spots = map_rows[pl.ds(source, 1), :] // PEERS
            chosen = lax.broadcasted_iota(jnp.int32, (ROWS, ROWS), 0) == spots
            rows = jnp.dot(
                chosen.astype(jnp.bfloat16),
                attended[slot_of[residue]],
                preferred_element_type=jnp.float32,
            )
            placed[pl.ds(residue, ROWS, stride=PEERS), :] = rows
            return carry
        lax.fori_loop(0, PEERS, place, 0, unroll=8)

        def hand_over(step):
            token_peer = behind(me, step)
            rows = placed[pl.ds(pl.multiple_of(token_peer * ROWS, ROWS), ROWS), :]
            ordered[step] = rows.astype(jnp.bfloat16)
            hint_copy(step).start()
        each(0, PEERS, hand_over, unroll=8)

    whole(queries, 1, PEERS - 1, Q_SENT, q_got.at[0]).wait_send()

    def finish(step, rows):
        cols = columns(ahead(me, step))
        total = stream[:, cols].astype(jnp.float32) + rows.astype(jnp.float32)
        out[:, cols] = total.astype(jnp.bfloat16)

    finish(0, attended[0])
    whole(landed, 1, PAIR - 1, BACK_SENT, back_got.at[0]).wait_recv()
    each(1, PAIR, lambda i: finish(i, landed[i]))

    def finish_block(block):
        whole(landed, block * PAIR, PAIR, BACK_SENT, back_got.at[block]).wait_recv()
        for step in (block * PAIR, block * PAIR + 1):
            finish(step, landed[step])
    each(1, blocks, finish_block)

    whole(attended, 1, PEERS - 1, BACK_SENT, back_got.at[0]).wait_send()

    @pl.when(grp == 0)
    def _():
        whole(ordered, 0, PEERS, HINT_SENT, bulk.at[HINT_GOT]).wait_send()


def local(qkv, hidden, row_map, frame_flags):
    planes = jnp.transpose(qkv[0], (1, 0, 2))
    cells = row_map.reshape(PEERS, ROWS)
    wide = PEERS * HEAD
    pairs = PEERS * TOKENS * HEAD * ROWS
    result = pl.pallas_call(
        kernel,
        out_shape=pltpu.VMEM((ROWS, wide), jnp.bfloat16),
        in_specs=[
            pl.BlockSpec(memory_space=pl.ANY),
            pl.BlockSpec(memory_space=pl.ANY),
            pl.BlockSpec(memory_space=pl.ANY),
            pl.BlockSpec(memory_space=pl.ANY),
        ],
        out_specs=pl.BlockSpec(memory_space=pltpu.VMEM),
        scratch_shapes=[
            pltpu.VMEM((PEERS, ROWS, HEAD), jnp.bfloat16),
            pltpu.VMEM((PEERS, ROWS, HEAD), jnp.bfloat16),
            pltpu.VMEM((PEERS, ROWS, HEAD), jnp.bfloat16),
            pltpu.VMEM((BLOCK, TOKENS), jnp.float32),
            pltpu.VMEM((BLOCK, TOKENS), jnp.float32),
            pltpu.VMEM((BLOCK, 128), jnp.float32),
            pltpu.VMEM((PEERS, ROWS, HEAD), jnp.bfloat16),
            pltpu.VMEM((PEERS, ROWS, HEAD), jnp.bfloat16),
            pltpu.VMEM((PEERS, ROWS, HEAD), jnp.bfloat16),
            pltpu.VMEM((TOKENS + PEERS, HEAD), jnp.float32),
            pltpu.VMEM((PEERS, ROWS, HEAD), jnp.bfloat16),
            pltpu.VMEM((ROWS, wide), jnp.bfloat16),
            pltpu.SMEM((FRAMES,), jnp.int32),
            pltpu.VMEM((PEERS, ROWS), jnp.int32),
            pltpu.SMEM((PEERS, ROWS), jnp.int32),
            pltpu.SMEM((PEERS,), jnp.int32),
            pltpu.SMEM((PEERS,), jnp.int32),
            pltpu.SemaphoreType.DMA((9,)),
            pltpu.SemaphoreType.DMA((PEERS // PAIR,)),
            pltpu.SemaphoreType.DMA((PEERS // PAIR,)),
            pltpu.SemaphoreType.DMA((7,)),
            pltpu.SemaphoreType.REGULAR,
        ],
        compiler_params=pltpu.CompilerParams(
            collective_id=0, has_side_effects=True, vmem_limit_bytes=60 * 1024 * 1024
        ),
        cost_estimate=pl.CostEstimate(
            flops=4 * pairs, bytes_accessed=6 * ROWS * wide * 2, transcendentals=TOKENS * TOKENS
        ),
        name="attend_and_exchange",
    )(planes, hidden[0], cells, frame_flags)
    return result[None]


def solution(mesh):
    in_specs = (
        P("grp", ("rep", "seq"), None, None),
        P("grp", ("rep", "seq"), None),
        P("rep"),
        P("rep"),
    )
    out_specs = P("grp", ("rep", "seq"), None)
    return jax.shard_map(local, mesh=mesh, in_specs=in_specs, out_specs=out_specs, check_vma=False)
```

```python
import math

import jax
import jax.numpy as jnp
from jax import lax
from jax.experimental import pallas as pl
from jax.experimental.pallas import tpu as pltpu
from jax.sharding import PartitionSpec as P

HEAD = 128
ROWS = 128
PEERS = 32
ZS = 8
YS = 4
TOKENS = ROWS * PEERS
FRAMES = 4
PAIR = 2
BLOCK = PAIR * ROWS
CHUNK = 512
LEAD = 14
HELD = 10
LEAD_SENT, K_SENT, V_SENT, Q_SENT, BACK_SENT, HINT_SENT, K_GOT, V_GOT, HINT_GOT = range(9)
SCALE = HEAD ** -0.5 * math.log2(math.e)
MESH = pl.DeviceIdType.MESH
LAST_DIMS = (((1,), (1,)), ((), ()))


def offset(step):
    turn = lax.rem(step, ZS)
    dz = jnp.where(lax.rem(turn, 2) == 1, ZS - (turn + 1) // 2, turn // 2)
    return dz, step // ZS


def ahead(me, step):
    dz, dy = offset(step)
    return lax.rem(me // YS + dz, ZS) * YS + lax.rem(lax.rem(me, YS) + dy, YS)


def behind(me, step):
    dz, dy = offset(step)
    return lax.rem(me // YS + ZS - dz, ZS) * YS + lax.rem(lax.rem(me, YS) + YS - dy, YS)


def columns(peer):
    return pl.ds(pl.multiple_of(peer * HEAD, HEAD), HEAD)


def score(queries, keys, scores, peak):
    highest = jnp.full((BLOCK, 128), -jnp.inf, jnp.float32)
    for start in range(0, TOKENS, CHUNK):
        part = lax.dot_general(
            queries, keys[pl.ds(start, CHUNK), :], LAST_DIMS, preferred_element_type=jnp.float32
        )
        scores[:, pl.ds(start, CHUNK)] = part
        for lane in range(0, CHUNK, 128):
            highest = jnp.maximum(highest, part[:, lane:lane + 128])
    peak[...] = jnp.broadcast_to(jnp.max(highest, axis=1, keepdims=True), (BLOCK, 128))


def blend(values, scores, peak, queries=None, keys=None, next_scores=None):
    level = peak[...]
    totals = jnp.zeros((BLOCK, 128), jnp.float32)
    blended = jnp.zeros((BLOCK, HEAD), jnp.float32)
    highest = jnp.full((BLOCK, 128), -jnp.inf, jnp.float32)
    for start in range(0, TOKENS, CHUNK):
        if queries is not None:
            part = lax.dot_general(
                queries, keys[pl.ds(start, CHUNK), :], LAST_DIMS, preferred_element_type=jnp.float32
            )
        rounded = []
        for lane in range(0, CHUNK, 128):
            weights = jnp.exp2((scores[:, pl.ds(start + lane, 128)] - level) * SCALE)
            totals = totals + weights
            rounded.append(weights.astype(jnp.bfloat16))
        if queries is not None:
            next_scores[:, pl.ds(start, CHUNK)] = part
            for lane in range(0, CHUNK, 128):
                highest = jnp.maximum(highest, part[:, lane:lane + 128])
        blended = blended + jnp.dot(
            jnp.concatenate(rounded, axis=1),
            values[pl.ds(start, CHUNK), :],
            preferred_element_type=jnp.float32,
        )
    if queries is not None:
        peak[...] = jnp.broadcast_to(jnp.max(highest, axis=1, keepdims=True), (BLOCK, 128))
    return (blended / jnp.sum(totals, axis=1, keepdims=True)).astype(jnp.bfloat16)


def kernel(
    qkv, hidden, row_map, frame_flags, out,
    keys, values, queries, even, odd, peak, attended, ordered, hint, placed, landed, stream,
    flags, map_rows, map_cells, owner_of, slot_of,
    bulk, q_got, back_got, local_sem, turn,
):
    grp = lax.axis_index("grp")
    me = lax.axis_index("seq")

    def push(src, dst, sent, got, **device):
        return pltpu.make_async_remote_copy(
            src_ref=src, dst_ref=dst, send_sem=bulk.at[sent], recv_sem=got,
            device_id=device, device_id_type=MESH,
        )

    def key_copy(step, sent):
        peer = ahead(me, step)
        return push(qkv.at[1, :, columns(peer)], keys.at[step], sent, bulk.at[K_GOT], seq=peer)

    def value_copy(step):
        peer = ahead(me, step)
        return push(qkv.at[2, :, columns(peer)], values.at[step], V_SENT, bulk.at[V_GOT], seq=peer)

    def query_copy(step):
        peer = ahead(me, step)
        return push(
            qkv.at[0, :, columns(peer)], queries.at[step], Q_SENT, q_got.at[step // PAIR], seq=peer
        )

    def back_copy(step):
        return push(
            attended.at[step], landed.at[step], BACK_SENT, back_got.at[step // PAIR], seq=behind(me, step)
        )

    def hint_copy(step):
        return push(ordered.at[step], hint.at[step], HINT_SENT, bulk.at[HINT_GOT], grp=1 - grp)

    def whole(ref, first, count, sent, got):
        part = ref.at[pl.ds(first, count)]
        return push(part, part, sent, got, seq=ahead(me, 1))

    def each(first, last, body, unroll=1):
        def step(i, carry):
            body(i)
            return carry
        lax.fori_loop(first, last, step, 0, unroll=unroll)

    own = [
        pltpu.make_async_copy(qkv.at[1, :, columns(me)], keys.at[0], local_sem.at[0]),
        pltpu.make_async_copy(qkv.at[2, :, columns(me)], values.at[0], local_sem.at[1]),
        pltpu.make_async_copy(qkv.at[0, :, columns(me)], queries.at[0], local_sem.at[2]),
        pltpu.make_async_copy(hidden, stream, local_sem.at[3]),
        pltpu.make_async_copy(row_map, map_rows, local_sem.at[4]),
        pltpu.make_async_copy(row_map, map_cells, local_sem.at[5]),
        pltpu.make_async_copy(frame_flags, flags, local_sem.at[6]),
    ]
    barrier = pltpu.get_barrier_semaphore()
    each(1, PEERS, lambda i: pl.semaphore_signal(
        barrier, inc=1, device_id={"seq": ahead(me, i)}, device_id_type=MESH), unroll=8)
    pl.semaphore_signal(barrier, inc=1, device_id={"grp": 1 - grp}, device_id_type=MESH)
    pl.semaphore_wait(barrier, PEERS)

    def send_keys_values():
        each(1, 1 + LEAD, lambda i: key_copy(i, LEAD_SENT).start(), unroll=7)
        each(1 + LEAD, PEERS, lambda i: key_copy(i, K_SENT).start(), unroll=8)
        each(1, PEERS, lambda i: value_copy(i).start(), unroll=8)

    @pl.when(grp == 0)
    def _():
        send_keys_values()
        for copy in own:
            copy.start()

        def find(residue):
            def look(c, found):
                return jnp.where(lax.rem(map_cells[c, 0], PEERS) == residue, c, found)
            source = lax.fori_loop(0, PEERS, look, 0)
            dz = lax.rem(me // YS + ZS - source // YS, ZS)
            dy = lax.rem(lax.rem(me, YS) + YS - lax.rem(source, YS), YS)
            owner_of[residue] = source
            slot_of[residue] = dy * ZS + jnp.where(dz < ZS // 2, 2 * dz, 2 * ZS - 1 - 2 * dz)

        whole(keys, 1, LEAD, LEAD_SENT, bulk.at[K_GOT]).wait_send()
        pl.semaphore_signal(turn, inc=1, device_id={"grp": 1}, device_id_type=MESH)
        own[5].wait()
        each(0, PEERS, find)

    @pl.when(grp == 1)
    def _():
        for copy in own:
            copy.start()
        pl.semaphore_wait(turn, 1)
        send_keys_values()
        whole(keys, 1, LEAD, LEAD_SENT, bulk.at[K_GOT]).wait_send()
        own[5].wait()

    whole(keys, 1 + LEAD, PEERS - 1 - LEAD, K_SENT, bulk.at[K_GOT]).wait_send()
    whole(values, 1, PEERS - 1, V_SENT, bulk.at[V_GOT]).wait_send()
    each(1, PEERS, lambda i: query_copy(i).start(), unroll=8)
    for copy in own[:5] + own[6:]:
        copy.wait()
    whole(keys, 1, PEERS - 1, K_SENT, bulk.at[K_GOT]).wait_recv()
    whole(values, 1, PEERS - 1, V_SENT, bulk.at[V_GOT]).wait_recv()

    flat_keys = keys.reshape(TOKENS, HEAD)
    flat_values = values.reshape(TOKENS, HEAD)
    blocks = PEERS // PAIR

    def query_rows(block):
        whole(queries, block * PAIR, PAIR, Q_SENT, q_got.at[block]).wait_recv()
        return queries[pl.ds(block * PAIR, PAIR)].reshape(BLOCK, HEAD)

    def give_back(step):
        @pl.when(step > 0)
        def _():
            back_copy(step).start()

    def add_hint(step):
        token_peer = behind(me, step)
        gate = flags[token_peer // (PEERS // FRAMES)].astype(jnp.float32)
        total = attended[step].astype(jnp.float32) + gate * hint[step].astype(jnp.float32)
        attended[step] = total.astype(jnp.bfloat16)
        give_back(step)

    def deliver(block, result):
        first = block * PAIR
        attended[pl.ds(first, PAIR)] = result.reshape(PAIR, ROWS, HEAD)

        @pl.when(grp == 0)
        def _():
            for step in (first, first + 1):
                give_back(step)

        @pl.when(jnp.logical_and(grp == 1, block + 1 == HELD))
        def _():
            whole(hint, 0, PEERS, HINT_SENT, bulk.at[HINT_GOT]).wait_recv()
            each(0, HELD * PAIR, add_hint, unroll=4)

        @pl.when(jnp.logical_and(grp == 1, block + 1 > HELD))
        def _():
            for step in (first, first + 1):
                add_hint(step)

    def work(block):
        rows = query_rows(block + 1)

        @pl.when(lax.rem(block, 2) == 0)
        def _():
            deliver(block, blend(flat_values, even, peak, rows, flat_keys, odd))

        @pl.when(lax.rem(block, 2) == 1)
        def _():
            deliver(block, blend(flat_values, odd, peak, rows, flat_keys, even))

    whole(queries, 1, PAIR - 1, Q_SENT, q_got.at[0]).wait_recv()
    score(queries[pl.ds(0, PAIR)].reshape(BLOCK, HEAD), flat_keys, even, peak)
    each(0, blocks - 1, work)
    deliver(blocks - 1, blend(flat_values, odd, peak))

    @pl.when(grp == 0)
    def _():
        def place(residue, carry):
            source = owner_of[residue]
            spots = map_rows[pl.ds(source, 1), :] // PEERS
            chosen = lax.broadcasted_iota(jnp.int32, (ROWS, ROWS), 0) == spots
            rows = jnp.dot(
                chosen.astype(jnp.bfloat16),
                attended[slot_of[residue]],
                preferred_element_type=jnp.float32,
            )
            placed[pl.ds(residue, ROWS, stride=PEERS), :] = rows
            return carry
        lax.fori_loop(0, PEERS, place, 0, unroll=16)

        def hand_over(step):
            token_peer = behind(me, step)
            rows = placed[pl.ds(pl.multiple_of(token_peer * ROWS, ROWS), ROWS), :]
            ordered[step] = rows.astype(jnp.bfloat16)
            hint_copy(step).start()
        each(0, PEERS, hand_over, unroll=8)

    whole(queries, 1, PEERS - 1, Q_SENT, q_got.at[0]).wait_send()

    def finish(step, rows):
        cols = columns(ahead(me, step))
        total = stream[:, cols].astype(jnp.float32) + rows.astype(jnp.float32)
        out[:, cols] = total.astype(jnp.bfloat16)

    finish(0, attended[0])
    whole(landed, 1, PAIR - 1, BACK_SENT, back_got.at[0]).wait_recv()
    each(1, PAIR, lambda i: finish(i, landed[i]))

    def finish_block(block):
        whole(landed, block * PAIR, PAIR, BACK_SENT, back_got.at[block]).wait_recv()
        for step in (block * PAIR, block * PAIR + 1):
            finish(step, landed[step])
    each(1, blocks, finish_block, unroll=5)

    whole(attended, 1, PEERS - 1, BACK_SENT, back_got.at[0]).wait_send()

    @pl.when(grp == 0)
    def _():
        whole(ordered, 0, PEERS, HINT_SENT, bulk.at[HINT_GOT]).wait_send()


def local(qkv, hidden, row_map, frame_flags):
    planes = jnp.transpose(qkv[0], (1, 0, 2))
    cells = row_map.reshape(PEERS, ROWS)
    wide = PEERS * HEAD
    pairs = PEERS * TOKENS * HEAD * ROWS
    result = pl.pallas_call(
        kernel,
        out_shape=pltpu.VMEM((ROWS, wide), jnp.bfloat16),
        in_specs=[
            pl.BlockSpec(memory_space=pl.ANY),
            pl.BlockSpec(memory_space=pl.ANY),
            pl.BlockSpec(memory_space=pl.ANY),
            pl.BlockSpec(memory_space=pl.ANY),
        ],
        out_specs=pl.BlockSpec(memory_space=pltpu.VMEM),
        scratch_shapes=[
            pltpu.VMEM((PEERS, ROWS, HEAD), jnp.bfloat16),
            pltpu.VMEM((PEERS, ROWS, HEAD), jnp.bfloat16),
            pltpu.VMEM((PEERS, ROWS, HEAD), jnp.bfloat16),
            pltpu.VMEM((BLOCK, TOKENS), jnp.float32),
            pltpu.VMEM((BLOCK, TOKENS), jnp.float32),
            pltpu.VMEM((BLOCK, 128), jnp.float32),
            pltpu.VMEM((PEERS, ROWS, HEAD), jnp.bfloat16),
            pltpu.VMEM((PEERS, ROWS, HEAD), jnp.bfloat16),
            pltpu.VMEM((PEERS, ROWS, HEAD), jnp.bfloat16),
            pltpu.VMEM((TOKENS + PEERS, HEAD), jnp.float32),
            pltpu.VMEM((PEERS, ROWS, HEAD), jnp.bfloat16),
            pltpu.VMEM((ROWS, wide), jnp.bfloat16),
            pltpu.SMEM((FRAMES,), jnp.int32),
            pltpu.VMEM((PEERS, ROWS), jnp.int32),
            pltpu.SMEM((PEERS, ROWS), jnp.int32),
            pltpu.SMEM((PEERS,), jnp.int32),
            pltpu.SMEM((PEERS,), jnp.int32),
            pltpu.SemaphoreType.DMA((9,)),
            pltpu.SemaphoreType.DMA((PEERS // PAIR,)),
            pltpu.SemaphoreType.DMA((PEERS // PAIR,)),
            pltpu.SemaphoreType.DMA((7,)),
            pltpu.SemaphoreType.REGULAR,
        ],
        compiler_params=pltpu.CompilerParams(
            collective_id=0, has_side_effects=True, vmem_limit_bytes=60 * 1024 * 1024
        ),
        cost_estimate=pl.CostEstimate(
            flops=4 * pairs, bytes_accessed=6 * ROWS * wide * 2, transcendentals=TOKENS * TOKENS
        ),
        name="attend_and_exchange",
    )(planes, hidden[0], cells, frame_flags)
    return result[None]


def solution(mesh):
    in_specs = (
        P("grp", ("rep", "seq"), None, None),
        P("grp", ("rep", "seq"), None),
        P("rep"),
        P("rep"),
    )
    out_specs = P("grp", ("rep", "seq"), None)
    return jax.shard_map(local, mesh=mesh, in_specs=in_specs, out_specs=out_specs, check_vma=False)
```
